32 devices in a mesh: groups: 2 (over y), seg: 16 (over z, x, core).
Axes of the slice: x: 2, y: 2, z: 4, core: 2. Of those that a mesh axis runs over, the one named last changes fastest.
Arguments:
- queries: bfloat16 [16384, 4096], P(('groups', 'seg')), parts along dimension 0, may hold values from -320 to 320
- keys: bfloat16 [16384, 1024], P(('groups', 'seg')), parts along dimension 0, may hold values from -60 to 60
- values: bfloat16 [16384, 1024], P(('groups', 'seg')), parts along dimension 0, may hold values from -14 to 14
Outputs:
- attended: bfloat16 [16384, 4096], P(('groups', 'seg')), parts along dimension 0
The draws below stay inside these ranges and needn't reach their ends.
There are 2 independent parts, one for each index of `groups`. The reference program is written for one: setup_inputs(seed, part) draws one part's arguments, and reference() takes and returns one part's arrays. A program takes and returns all parts, laid end to end along the dimension named above; each array names one. Nothing has to cross between parts.
All inputs are finite; a program needn't handle non-finite values.
Results may differ from the reference program's by a relative error of at most 0.0036.
Values may be sent and summed in bfloat16 or wider, within the bound.
A program may use at most 128 MiB of HBM per device.

```python
import math
import jax
import jax.numpy as jnp
from jax import lax

QH = 32
KVH = 8
DH = 128
SEG_LEN = 1024
TOKENS = 8192


def shared_keys(key):
    sub = jax.random.fold_in(key, 11)
    key_noise = jax.random.fold_in(sub, 0)
    base_keys = jnp.clip(jax.random.normal(key_noise, (TOKENS, KVH * DH), jnp.float32), -6.0, 6.0)
    positions = jnp.arange(TOKENS)
    rising = 1.0 + 2.0 * positions.astype(jnp.float32) / TOKENS
    base_keys = base_keys * rising[:, None]
    return base_keys


def draw_keys(key, part):
    base_keys = shared_keys(key)
    return base_keys.astype(jnp.bfloat16)


def draw_queries(key, part):
    sub = jax.random.fold_in(key, 23)
    key_noise = jax.random.fold_in(sub, 0)
    noise = jnp.clip(jax.random.normal(key_noise, (TOKENS, QH * DH), jnp.float32), -6.0, 6.0)
    return jnp.clip(noise, -320.0, 320.0).astype(jnp.bfloat16)


def draw_values(key, part):
    sub = jax.random.fold_in(key, 31)
    key_noise, key_offset = jax.random.split(sub, 2)
    offsets = jnp.clip(jax.random.normal(key_offset, (TOKENS // SEG_LEN, KVH * DH), jnp.float32), -4.0, 4.0) * 2.0
    offset_rows = jnp.repeat(offsets, SEG_LEN, axis=0, total_repeat_length=TOKENS)
    noise = jnp.clip(jax.random.normal(key_noise, (TOKENS, KVH * DH), jnp.float32), -6.0, 6.0)
    return (noise + offset_rows).astype(jnp.bfloat16)


def setup_inputs(seed: int = 0, part: int = 0) -> dict:
    key_of = jax.random.split(jax.random.key(seed), 4)
    part_splits = jax.random.split(jax.random.fold_in(key_of[3], part), 4)
    return {
        "queries": draw_queries(jax.random.fold_in(jax.random.fold_in(key_of[3], part), 71), part),
        "keys": draw_keys(jax.random.fold_in(jax.random.fold_in(key_of[3], part), 71), part),
        "values": draw_values(jax.random.fold_in(jax.random.fold_in(key_of[3], part), 71), part),
    }


def features(block):
    return (jax.nn.elu(block.astype(jnp.float32)) + 1.0).astype(jnp.bfloat16)

def reference(queries, keys, values):
    segment_count = queries.shape[0] // SEG_LEN
    group_size = QH // KVH
    query_segs = queries.reshape(segment_count, SEG_LEN, KVH, group_size, DH)
    key_segs = keys.reshape(segment_count, SEG_LEN, KVH, DH)
    value_segs = values.reshape(segment_count, SEG_LEN, KVH, DH)
    key_feat = features(key_segs).astype(jnp.float32)
    memory_delta = jnp.einsum('sthd,sthe->shde', key_feat, value_segs.astype(jnp.float32))
    norm_delta = lax.optimization_barrier(jnp.sum(key_feat, axis=1))
    memory_before = jnp.concatenate([jnp.zeros_like(memory_delta[:1]), jnp.cumsum(memory_delta, axis=0)[:-1]], 0)
    norm_before = jnp.concatenate([jnp.zeros_like(norm_delta[:1]), jnp.cumsum(norm_delta, axis=0)[:-1]], 0)
    causal = jnp.tril(jnp.ones((SEG_LEN, SEG_LEN), dtype=bool))

    def one_segment(pieces):
        query_block, key_block, value_block, mem_block, norm_block = pieces
        scores = jnp.einsum('tgjd,ugd->gjtu', query_block.astype(jnp.float32), key_block.astype(jnp.float32)) / math.sqrt(DH)
        scores = jnp.where(causal[None, None], scores, -1e+30)
        row_max = lax.optimization_barrier(jnp.max(scores, axis=-1, keepdims=True))
        weights_raw = jnp.exp(scores - row_max)
        row_total = lax.optimization_barrier(jnp.sum(weights_raw, axis=-1, keepdims=True))
        weights = (weights_raw / row_total).astype(jnp.bfloat16)
        local_out = jnp.einsum('gjtu,ugd->tgjd', weights.astype(jnp.float32), value_block.astype(jnp.float32))
        query_feat = features(query_block).astype(jnp.float32)
        numerator = jnp.einsum('tgjd,gde->tgje', query_feat, mem_block, precision=lax.Precision.HIGHEST)
        denominator = jnp.einsum('tgjd,gd->tgj', query_feat, norm_block, precision=lax.Precision.HIGHEST)
        mem_read = numerator / jnp.maximum(denominator, 1.0)[..., None]
        joined = 0.5 * (local_out + mem_read)
        return joined.reshape(SEG_LEN, QH * DH).astype(jnp.bfloat16)
    result = lax.map(one_segment, (query_segs, key_segs, value_segs, memory_before, norm_before))
    return result.reshape(segment_count * SEG_LEN, QH * DH)
```

```python
import functools
import math

import jax
import jax.numpy as jnp
from jax import lax
from jax.experimental import pallas as pl
from jax.experimental.pallas import tpu as pltpu
from jax.sharding import PartitionSpec as P

QH = 32
KVH = 8
DH = 128
GROUP = QH // KVH
HALF = KVH // 2
WIDTH = GROUP * DH
NORM_ROWS = 16
BLOCK = 256
MESH = pl.DeviceIdType.MESH
LAST = (((1,), (1,)), ((), ()))
FIRST = (((0,), (0,)), ((), ()))


def features(x):
    x = x.astype(jnp.float32)
    return jnp.where(x > 0, x + 1.0, jnp.exp(x)).astype(jnp.bfloat16)


def kernel(
    steps, rows,
    q_ref, k_ref, v_ref, out_ref,
    q_s, k_s, v_s, loc_s, o_s, total, before, snd, rcv, memaug,
    own_sem, q_send, q_recv, kv_send, kv_recv, m_send, m_recv, o_own, o_send, o_recv,
):
    me = lax.axis_index("seg")
    side = me % 2
    seg = me // 2
    other = 1 - side
    mate = me + 1 - 2 * side
    peers, bits = [], []
    for t in range(steps):
        bit = (seg // 2**t) % 2
        bits.append(bit)
        peers.append((seg + (1 - 2 * bit) * 2**t) * 2 + side)

    barrier = pltpu.get_barrier_semaphore()
    for d in [mate] + peers:
        pl.semaphore_signal(barrier, inc=1, device_id={"seg": d}, device_id_type=MESH)

    my_rows = pl.ds(pl.multiple_of(side * rows, rows), rows)
    mate_rows = pl.ds(pl.multiple_of(other * rows, rows), rows)

    def cols(which, width, g=0, size=None):
        start = which * (HALF * width) + g * width
        return pl.ds(pl.multiple_of(start, 128), size or width)

    own = []
    for n, (src, dst) in enumerate(((k_ref, k_s), (v_ref, v_s))):
        own.append(pltpu.make_async_copy(
            src.at[:, cols(side, DH, 0, HALF * DH)], dst.at[my_rows, :], own_sem.at[n]))
    for g in range(HALF):
        own.append(pltpu.make_async_copy(
            q_ref.at[:, cols(side, WIDTH, g)], q_s.at[g, my_rows, :], own_sem.at[2 + g]))
    for c in own:
        c.start()
    pl.semaphore_wait(barrier, 1 + steps)

    def remote(src, dst, s, r, dev):
        return pltpu.make_async_remote_copy(
            src_ref=src, dst_ref=dst, send_sem=s, recv_sem=r,
            device_id={"seg": dev}, device_id_type=MESH)

    kv = []
    for n, (src, dst) in enumerate(((k_ref, k_s), (v_ref, v_s))):
        kv.append(remote(src.at[:, cols(other, DH, 0, HALF * DH)], dst.at[my_rows, :],
                         kv_send.at[n], kv_recv.at[n], mate))
    qs = []
    for g in range(HALF):
        qs.append(remote(q_ref.at[:, cols(other, WIDTH, g)], q_s.at[g, my_rows, :],
                         q_send.at[g], q_recv.at[g], mate))
    for c in kv + qs:
        c.start()

    own[0].wait()
    own[1].wait()
    kv[0].wait_recv()
    kv[1].wait_recv()

    seg_rows = 2 * rows
    ones_rows = jnp.ones((NORM_ROWS, seg_rows), jnp.bfloat16)
    for g in range(HALF):
        kf = features(k_s[:, g * DH:(g + 1) * DH])
        total[g, 0:DH, :] = lax.dot_general(
            kf, v_s[:, g * DH:(g + 1) * DH], FIRST, preferred_element_type=jnp.float32)
        total[g, DH:, :] = jnp.dot(ones_rows, kf, preferred_element_type=jnp.float32)
    before[...] = jnp.zeros_like(before)

    def send_total(t):
        snd[t] = total[...].astype(jnp.bfloat16)
        copy = remote(snd.at[t], rcv.at[t], m_send.at[t], m_recv.at[t], peers[t])
        copy.start()
        return copy

    sums = []
    if steps:
        sums.append(send_total(0))

    def take_total(t):
        sums[t].wait_recv()
        got = rcv[t].astype(jnp.float32)
        before[...] += got * bits[t].astype(jnp.float32)
        if t + 1 < steps:
            total[...] += got
            sums.append(send_total(t + 1))

    scale = math.log2(math.e) / math.sqrt(DH)
    lower = (lax.broadcasted_iota(jnp.int32, (BLOCK, BLOCK), 1)
             <= lax.broadcasted_iota(jnp.int32, (BLOCK, BLOCK), 0))

    def local(g):
        def head(j, _):
            at = pl.ds(pl.multiple_of(j * DH, DH), DH)
            for i in range(seg_rows // BLOCK):
                lo = i * BLOCK
                here = slice(lo, lo + BLOCK)
                q = q_s[g, here, at]
                gc = slice(g * DH, (g + 1) * DH)
                ones = jnp.ones((BLOCK, DH), jnp.bfloat16)
                sd = lax.dot_general(q, k_s[here, gc], LAST, preferred_element_type=jnp.float32)
                sd = jnp.where(lower, sd, -1e30)
                top = jnp.max(sd, axis=-1, keepdims=True)
                if i:
                    so = lax.dot_general(
                        q, k_s[0:lo, gc], LAST, preferred_element_type=jnp.float32)
                    top = jnp.maximum(top, jnp.max(so, axis=-1, keepdims=True))
                pd = jnp.exp2((sd - top) * scale).astype(jnp.bfloat16)
                acc = jnp.dot(pd, jnp.concatenate([v_s[here, gc], ones], 1),
                              preferred_element_type=jnp.float32)
                if i:
                    po = jnp.exp2((so - top) * scale).astype(jnp.bfloat16)
                    ones = jnp.ones((lo, DH), jnp.bfloat16)
                    acc += jnp.dot(po, jnp.concatenate([v_s[0:lo, gc], ones], 1),
                                   preferred_element_type=jnp.float32)
                loc_s[g, here, at] = acc[:, :DH] / acc[:, DH:]
            return 0
        lax.fori_loop(0, GROUP, head, 0)

    def prepare():
        for g in range(HALF):
            full = before[g]
            norm = jnp.broadcast_to(full[DH:DH + 1, :], (DH, DH)).T
            both = jnp.concatenate([full[:DH, :], norm], 1)
            high = both.astype(jnp.bfloat16)
            memaug[g, 0:DH, :] = high
            memaug[g, DH:, :] = (both - high.astype(jnp.float32)).astype(jnp.bfloat16)

    outs = []

    def finish(g):
        def head(j, _):
            at = pl.ds(pl.multiple_of(j * DH, DH), DH)
            for i in range(seg_rows // BLOCK):
                here = slice(i * BLOCK, (i + 1) * BLOCK)
                qf = features(q_s[g, here, at])
                r = jnp.dot(jnp.concatenate([qf, qf], 1), memaug[g],
                            preferred_element_type=jnp.float32)
                read = r[:, :DH] / jnp.maximum(r[:, DH:], 1.0)
                o_s[g, here, at] = (0.5 * (loc_s[g, here, at] + read)).astype(jnp.bfloat16)
            return 0
        lax.fori_loop(0, GROUP, head, 0)
        there = out_ref.at[:, cols(side, WIDTH, g)]
        far = remote(o_s.at[g, mate_rows, :], there, o_send.at[g], o_recv.at[g], mate)
        far.start()
        near = pltpu.make_async_copy(o_s.at[g, my_rows, :], there, o_own.at[g])
        near.start()
        outs.append((far, near))

    ready = HALF - 1
    each = -(-steps // ready)
    taken = 0
    for g in range(HALF):
        own[2 + g].wait()
        qs[g].wait_recv()
        local(g)
        while taken < min(steps, (g + 1) * each):
            take_total(taken)
            taken += 1
        if g == ready - 1:
            prepare()
            for h in range(ready):
                finish(h)
        if g >= ready:
            finish(g)

    for c in kv + qs + sums:
        c.wait_send()
    for far, near in outs:
        near.wait()
        far.wait()


def solution(mesh):
    count = mesh.shape["seg"] // 2
    steps = count.bit_length() - 1
    assert count == 2**steps

    def on_device(queries, keys, values):
        rows = queries.shape[0]
        seg_rows = 2 * rows
        bf16, f32 = jnp.bfloat16, jnp.float32
        dma = pltpu.SemaphoreType.DMA
        slots = max(steps, 1)
        sums = (HALF, DH + NORM_ROWS, DH)
        return pl.pallas_call(
            functools.partial(kernel, steps, rows),
            out_shape=jax.ShapeDtypeStruct(queries.shape, bf16),
            in_specs=[pl.BlockSpec(memory_space=pl.ANY)] * 3,
            out_specs=pl.BlockSpec(memory_space=pl.ANY),
            scratch_shapes=[
                pltpu.VMEM((HALF, seg_rows, WIDTH), bf16),
                pltpu.VMEM((seg_rows, HALF * DH), bf16),
                pltpu.VMEM((seg_rows, HALF * DH), bf16),
                pltpu.VMEM((HALF, seg_rows, WIDTH), f32),
                pltpu.VMEM((HALF, seg_rows, WIDTH), bf16),
                pltpu.VMEM(sums, f32),
                pltpu.VMEM(sums, f32),
                pltpu.VMEM((slots,) + sums, bf16),
                pltpu.VMEM((slots,) + sums, bf16),
                pltpu.VMEM((HALF, 2 * DH, 2 * DH), bf16),
                dma((2 + HALF,)),
                dma((HALF,)), dma((HALF,)),
                dma((2,)), dma((2,)),
                dma((slots,)), dma((slots,)),
                dma((HALF,)), dma((HALF,)), dma((HALF,)),
            ],
            compiler_params=pltpu.CompilerParams(
                collective_id=0, has_side_effects=True, vmem_limit_bytes=52 * 2**20),
            cost_estimate=pl.CostEstimate(
                flops=4 * seg_rows * seg_rows * QH // 2 * DH,
                bytes_accessed=20 * rows * QH * DH // 2,
                transcendentals=seg_rows * seg_rows * QH // 4),
        )(queries, keys, values)

    return jax.shard_map(
        on_device,
        mesh=mesh,
        in_specs=(P(("groups", "seg"), None),) * 3,
        out_specs=P(("groups", "seg"), None),
        check_vma=False,
    )
```

```python
import functools
import math

import jax
import jax.numpy as jnp
from jax import lax
from jax.experimental import pallas as pl
from jax.experimental.pallas import tpu as pltpu
from jax.sharding import PartitionSpec as P

QH = 32
KVH = 8
DH = 128
GROUP = QH // KVH
HALF = KVH // 2
WIDTH = GROUP * DH
NORM_ROWS = 16
BLOCK = 256
PAIR = 2
MESH = pl.DeviceIdType.MESH
LAST = (((1,), (1,)), ((), ()))
FIRST = (((0,), (0,)), ((), ()))


def features(x):
    x = x.astype(jnp.float32)
    return jnp.where(x > 0, x + 1.0, jnp.exp(x)).astype(jnp.bfloat16)


def kernel(
    steps, rows,
    q_ref, k_ref, v_ref, out_ref,
    q_s, k_s, v_s, loc_s, o_s, total, before, snd, rcv, memaug,
    own_sem, q_send, q_recv, kv_send, kv_recv, m_send, m_recv, o_own, o_send, o_recv,
):
    me = lax.axis_index("seg")
    side = me % 2
    seg = me // 2
    other = 1 - side
    mate = me + 1 - 2 * side
    peers, bits = [], []
    for t in range(steps):
        bit = (seg // 2**t) % 2
        bits.append(bit)
        peers.append((seg + (1 - 2 * bit) * 2**t) * 2 + side)

    barrier = pltpu.get_barrier_semaphore()
    for d in [mate] + peers:
        pl.semaphore_signal(barrier, inc=1, device_id={"seg": d}, device_id_type=MESH)

    my_rows = pl.ds(pl.multiple_of(side * rows, rows), rows)
    mate_rows = pl.ds(pl.multiple_of(other * rows, rows), rows)

    def cols(which, width, g=0, size=None):
        start = which * (HALF * width) + g * width
        return pl.ds(pl.multiple_of(start, 128), size or width)

    own = []
    for n, (src, dst) in enumerate(((k_ref, k_s), (v_ref, v_s))):
        own.append(pltpu.make_async_copy(
            src.at[:, cols(side, DH, 0, HALF * DH)], dst.at[my_rows, :], own_sem.at[n]))
    for g in range(HALF):
        own.append(pltpu.make_async_copy(
            q_ref.at[:, cols(side, WIDTH, g)], q_s.at[g, my_rows, :], own_sem.at[2 + g]))
    for c in own:
        c.start()
    pl.semaphore_wait(barrier, 1 + steps)

    def remote(src, dst, s, r, dev):
        return pltpu.make_async_remote_copy(
            src_ref=src, dst_ref=dst, send_sem=s, recv_sem=r,
            device_id={"seg": dev}, device_id_type=MESH)

    kv = []
    for n, (src, dst) in enumerate(((k_ref, k_s), (v_ref, v_s))):
        kv.append(remote(src.at[:, cols(other, DH, 0, HALF * DH)], dst.at[my_rows, :],
                         kv_send.at[n], kv_recv.at[n], mate))
    qs = []
    for g in range(HALF):
        qs.append(remote(q_ref.at[:, cols(other, WIDTH, g)], q_s.at[g, my_rows, :],
                         q_send.at[g], q_recv.at[g], mate))
    for c in kv + qs:
        c.start()

    seg_rows = 2 * rows
    ones_rows = jnp.ones((NORM_ROWS, rows), jnp.bfloat16)

    def add_terms(part):
        for g in range(HALF):
            kf = features(k_s[part, g * DH:(g + 1) * DH])
            total[g, 0:DH, :] += lax.dot_general(
                kf, v_s[part, g * DH:(g + 1) * DH], FIRST, preferred_element_type=jnp.float32)
            total[g, DH:, :] += jnp.dot(ones_rows, kf, preferred_element_type=jnp.float32)

    before[...] = jnp.zeros_like(before)
    total[...] = jnp.zeros_like(total)
    own[0].wait()
    own[1].wait()
    add_terms(my_rows)
    kv[0].wait_recv()
    kv[1].wait_recv()
    add_terms(mate_rows)

    def send_total(t):
        snd[t] = total[...].astype(jnp.bfloat16)
        copy = remote(snd.at[t], rcv.at[t], m_send.at[t], m_recv.at[t], peers[t])
        copy.start()
        return copy

    sums = []
    if steps:
        sums.append(send_total(0))

    def take_total(t):
        sums[t].wait_recv()
        got = rcv[t].astype(jnp.float32)
        before[...] += got * bits[t].astype(jnp.float32)
        if t + 1 < steps:
            total[...] += got
            sums.append(send_total(t + 1))

    scale = math.log2(math.e) / math.sqrt(DH)
    shape = (PAIR * BLOCK, BLOCK)
    lower = (lax.broadcasted_iota(jnp.int32, shape, 1)
             <= lax.broadcasted_iota(jnp.int32, shape, 0) % BLOCK)

    def local(g):
        def heads(j, _):
            ats = [pl.ds(pl.multiple_of((j * PAIR + a) * DH, DH), DH) for a in range(PAIR)]
            for i in range(seg_rows // BLOCK):
                lo = i * BLOCK
                here = slice(lo, lo + BLOCK)
                q = jnp.concatenate([q_s[g, here, at] for at in ats], 0)
                gc = slice(g * DH, (g + 1) * DH)
                ones = jnp.ones((BLOCK, DH), jnp.bfloat16)
                sd = lax.dot_general(q, k_s[here, gc], LAST, preferred_element_type=jnp.float32)
                sd = jnp.where(lower, sd, -1e30)
                top = jnp.max(sd, axis=-1, keepdims=True)
                if i:
                    so = lax.dot_general(
                        q, k_s[0:lo, gc], LAST, preferred_element_type=jnp.float32)
                    top = jnp.maximum(top, jnp.max(so, axis=-1, keepdims=True))
                pd = jnp.exp2((sd - top) * scale).astype(jnp.bfloat16)
                acc = jnp.dot(pd, jnp.concatenate([v_s[here, gc], ones], 1),
                              preferred_element_type=jnp.float32)
                if i:
                    po = jnp.exp2((so - top) * scale).astype(jnp.bfloat16)
                    ones = jnp.ones((lo, DH), jnp.bfloat16)
                    acc += jnp.dot(po, jnp.concatenate([v_s[0:lo, gc], ones], 1),
                                   preferred_element_type=jnp.float32)
                for a in range(PAIR):
                    to = pl.ds(pl.multiple_of((j * PAIR + a) * 2 * DH, 2 * DH), 2 * DH)
                    loc_s[g, here, to] = acc[a * BLOCK:(a + 1) * BLOCK]
            return 0
        lax.fori_loop(0, GROUP // PAIR, heads, 0)

    def prepare():
        for g in range(HALF):
            full = before[g]
            norm = jnp.broadcast_to(full[DH:DH + 1, :], (DH, DH)).T
            both = jnp.concatenate([full[:DH, :], norm], 1)
            high = both.astype(jnp.bfloat16)
            memaug[g, 0:DH, :] = high
            memaug[g, DH:, :] = (both - high.astype(jnp.float32)).astype(jnp.bfloat16)

    outs = []

    def finish_rows(g, start):
        def head(j, _):
            at = pl.ds(pl.multiple_of(j * DH, DH), DH)
            for i in range(rows // BLOCK):
                here = pl.ds(pl.multiple_of(start + i * BLOCK, BLOCK), BLOCK)
                qf = features(q_s[g, here, at])
                r = jnp.dot(jnp.concatenate([qf, qf], 1), memaug[g],
                            preferred_element_type=jnp.float32)
                near = loc_s[g, here, pl.ds(pl.multiple_of(j * 2 * DH, 2 * DH), 2 * DH)]
                row, den = near[:, DH:], jnp.maximum(r[:, DH:], 1.0)
                both = (near[:, :DH] * den + r[:, :DH] * row) / (row * den)
                o_s[g, here, at] = (0.5 * both).astype(jnp.bfloat16)
            return 0
        lax.fori_loop(0, GROUP, head, 0)

    def finish(g):
        there = out_ref.at[:, cols(side, WIDTH, g)]
        finish_rows(g, other * rows)
        far = remote(o_s.at[g, mate_rows, :], there, o_send.at[g], o_recv.at[g], mate)
        far.start()
        finish_rows(g, side * rows)
        near = pltpu.make_async_copy(o_s.at[g, my_rows, :], there, o_own.at[g])
        near.start()
        outs.append((far, near))

    ready = HALF - 1
    each = -(-steps // ready)
    taken = 0
    for g in range(HALF):
        own[2 + g].wait()
        qs[g].wait_recv()
        local(g)
        while taken < min(steps, (g + 1) * each):
            take_total(taken)
            taken += 1
        if g == ready - 1:
            prepare()
            for h in range(ready):
                finish(h)
        if g >= ready:
            finish(g)

    for c in kv + qs + sums:
        c.wait_send()
    for far, near in outs:
        near.wait()
        far.wait()


def pass_on(parts, src_ref, dst_ref, held, in_sem, out_sem):
    size = held.shape[0] // parts
    loads, stores = [], []
    for n in range(parts):
        part = slice(n * size, (n + 1) * size)
        loads.append(pltpu.make_async_copy(src_ref.at[part, :], held.at[part, :], in_sem.at[n]))
        stores.append(pltpu.make_async_copy(held.at[part, :], dst_ref.at[part, :], out_sem.at[n]))
        loads[n].start()
    for n in range(parts):
        loads[n].wait()
        stores[n].start()
    for n in range(parts):
        stores[n].wait()


def solution(mesh):
    count = mesh.shape["seg"] // 2
    steps = count.bit_length() - 1
    assert count == 2**steps

    def on_device(queries, keys, values):
        rows = queries.shape[0]
        seg_rows = 2 * rows
        bf16, f32 = jnp.bfloat16, jnp.float32
        dma = pltpu.SemaphoreType.DMA
        slots = max(steps, 1)
        sums = (HALF, DH + NORM_ROWS, DH)
        joined = pl.pallas_call(
            functools.partial(kernel, steps, rows),
            out_shape=jax.ShapeDtypeStruct(queries.shape, bf16),
            in_specs=[pl.BlockSpec(memory_space=pl.ANY)] * 3,
            out_specs=pl.BlockSpec(memory_space=pl.ANY),
            scratch_shapes=[
                pltpu.VMEM((HALF, seg_rows, WIDTH), bf16),
                pltpu.VMEM((seg_rows, HALF * DH), bf16),
                pltpu.VMEM((seg_rows, HALF * DH), bf16),
                pltpu.VMEM((HALF, seg_rows, 2 * WIDTH), f32),
                pltpu.VMEM((HALF, seg_rows, WIDTH), bf16),
                pltpu.VMEM(sums, f32),
                pltpu.VMEM(sums, f32),
                pltpu.VMEM((slots,) + sums, bf16),
                pltpu.VMEM((slots,) + sums, bf16),
                pltpu.VMEM((HALF, 2 * DH, 2 * DH), bf16),
                dma((2 + HALF,)),
                dma((HALF,)), dma((HALF,)),
                dma((2,)), dma((2,)),
                dma((slots,)), dma((slots,)),
                dma((HALF,)), dma((HALF,)), dma((HALF,)),
            ],
            compiler_params=pltpu.CompilerParams(
                collective_id=0, has_side_effects=True, vmem_limit_bytes=60 * 2**20),
            cost_estimate=pl.CostEstimate(
                flops=4 * seg_rows * seg_rows * QH // 2 * DH,
                bytes_accessed=20 * rows * QH * DH // 2,
                transcendentals=seg_rows * seg_rows * QH // 4),
        )(queries, keys, values)
        parts = math.gcd(rows // 16, 16)
        return pl.pallas_call(
            functools.partial(pass_on, parts),
            out_shape=jax.ShapeDtypeStruct(joined.shape, bf16),
            in_specs=[pl.BlockSpec(memory_space=pl.ANY)],
            out_specs=pl.BlockSpec(memory_space=pl.ANY),
            scratch_shapes=[pltpu.VMEM(joined.shape, bf16), dma((parts,)), dma((parts,))],
            compiler_params=pltpu.CompilerParams(vmem_limit_bytes=60 * 2**20),
            cost_estimate=pl.CostEstimate(
                flops=0, bytes_accessed=4 * joined.size, transcendentals=0),
        )(joined)

    return jax.shard_map(
        on_device,
        mesh=mesh,
        in_specs=(P(("groups", "seg"), None),) * 3,
        out_specs=P(("groups", "seg"), None),
        check_vma=False,
    )
```
